32 devices in a mesh: pair: 8 (over z, y), grid: 4 (over x, core).
Axes of the slice: x: 2, y: 2, z: 4, core: 2. Of those that a mesh axis runs over, the one named last changes fastest.
Arguments:
- adjoint: bfloat16 [2048, 9, 2001], P(('pair', 'grid')), may hold values from -0.29882812 to 0.29882812
- first_block: int32 [2048, 1], P(('pair', 'grid')), may hold values from 0 to 31; in each aligned block of 64 rows (0 to 63, 64 to 127, ...) at most 3 rows name the same one
- second_station: int32 [2048], P(('pair', 'grid')), may hold values from 0 to 3999
- station_block: int32 [4000], replicated, may hold values from 0 to 31
- lag_lo: int32 [2048], P(('pair', 'grid')), may hold values from 0 to 999
- lag_hi: int32 [2048], P(('pair', 'grid')), may hold values from 1001 to 2001
- pair_count: int32 [32], P(('pair', 'grid')), may hold values from 1 to 64, 1536 in all
- green_function: bfloat16 [32, 3, 2, 512, 2048], P(None, None, None, 'pair', 'grid'), may hold values from -0.11 to 0.11
Outputs:
- kernel: float32 [2, 2048], P(None, 'grid')
The draws below stay inside these ranges and needn't reach their ends.
Inputs may be any that keep to these rules, and one draw needn't show every extreme that they name: `first_block`: in the rows of one device no block is named by more than 3 rows. Slots 0 to pair_count - 1 of a device hold live pairs, the others padding.
All inputs are finite; a program needn't handle non-finite values.
Results may differ from the reference program's by a relative error of at most 0.0047.
Values may be sent and summed in bfloat16 or wider, within the bound.
A program may use at most 128 MiB of HBM per device.

```python
import math
import jax
import jax.numpy as jnp
import numpy as np
from jax import lax

LAGS = 2001
NF = 256
BANDS = 2
BLOCKS = 32
STATIONS = 4000
ROWS = 64
CAPACITY = 3
PAIRS = 2048
POINTS = 2048
N_PAIR = 8
N_GRID = 4


def draw_green_function(key, part):
    key = jax.random.fold_in(key, 11)
    envelope_key, value_key = jax.random.split(key)
    full_shape = (BLOCKS, 3, 2, BANDS * NF, POINTS)
    envelope = jnp.exp(4.0 * jax.random.uniform(envelope_key, (BLOCKS, 1, 1, 1, POINTS), jnp.float32) - 3.0)
    values = jax.random.truncated_normal(value_key, -4.0, 4.0, full_shape, jnp.float32)
    return (0.01 * envelope * values).astype(jnp.bfloat16)


def with_ends(array, rng, least, high):
    longest = array.shape.index(max(array.shape))
    spots = []
    for shift in (0, 1):
        where = [jax.random.randint(jax.random.fold_in(rng, axis), (), 0, length) for axis, length in enumerate(array.shape)]
        where[longest] = (where[longest] + shift) % array.shape[longest]
        spots.append(tuple(where))
    return array.at[spots[0]].set(least).at[spots[1]].set(high)


def block_scale(stream_key, extent, pieces, low, top_value):
    gain, own = 1.0, jax.random.fold_in(stream_key, 6)
    for dim, shards_of in pieces:
        steps = jnp.exp(jax.random.uniform(jax.random.fold_in(own, dim), (shards_of,), jnp.float32, low / len(pieces), top_value / len(pieces)))
        gain = gain * jnp.repeat(steps, extent[dim] // shards_of).reshape([-1 if axis == dim else 1 for axis in range(len(extent))])
    return gain


def profile(count, total, bound, lean):
    loads = [(1 << 20) // math.isqrt(grade ** lean) + 1 for grade in range(2, count + 1)]
    rest, holding = total - bound - (count - 1), [1] * (count - 1)
    while rest > 0:
        candidates = [i for i in range(count - 1) if holding[i] < bound]
        whole, remaining = sum([loads[i] for i in candidates]), rest
        for i in candidates:
            addition = min(bound - holding[i], max(1, remaining * loads[i] // whole), rest)
            holding[i] = holding[i] + addition
            rest = rest - addition
    return np.array([bound] + holding)


def ragged_sizes(stream_key, count, total, most, slope):
    if count == 2:
        one = jax.random.randint(stream_key, (), max(1, total - most), min(most, total - 1) + 1)
        return jnp.stack([one, total - one])
    lengths = jnp.asarray(profile(count, total, most, slope), jnp.int32)
    couples = (count - 1) // 2
    giver, taker = lengths[1:1 + 2 * couples:2], lengths[2:2 + 2 * couples:2]
    slack = jnp.minimum(giver - 1, most - taker)
    moved = jax.random.randint(jax.random.fold_in(stream_key, 1), (couples,), 0, 1 << 20) % (slack + 1)
    lengths = lengths.at[1:1 + 2 * couples:2].set(giver - moved).at[2:2 + 2 * couples:2].set(taker + moved)
    return lengths[jax.random.permutation(jax.random.fold_in(stream_key, 2), count)]


def routed_block(key, own, number, rows, number_of, top, bound, slope):
    ranking = jax.random.permutation(key, number_of)
    crowded, ordinary = shares(number_of, rows * top, bound, slope, True), shares(number_of, rows * top, bound, slope, False)
    places = jnp.arange(number_of)

    def named(sizes, offset_by):
        used = int((sizes > 0).sum())
        fixed = max(1, used // 4)
        shifted = fixed + (places - fixed + offset_by * (used - fixed)) % max(1, number_of - fixed)
        return jnp.zeros((number_of,), jnp.int32).at[ranking[jnp.where(places < fixed, places, shifted)]].set(jnp.asarray(sizes, jnp.int32))

    sizes = jnp.where(number % 4 == 0, named(crowded, number // 4), named(ordinary, number - number // 4 - 1))
    mixed = jax.random.permutation(jax.random.fold_in(own, 3), number_of)
    source_of, sink = mixed[0:number_of // 2 * 2:2], mixed[1:number_of // 2 * 2:2]
    room = jnp.minimum(sizes[source_of] - 1, bound - sizes[sink]) // 2
    room = jnp.where((source_of == ranking[0]) | (sink == ranking[0]) | (sizes[sink] == 0), 0, jnp.maximum(room, 0))
    shifted = jax.random.randint(jax.random.fold_in(own, 4), (number_of // 2,), 0, 1 << 20) % (room + 1)
    sizes = sizes.at[source_of].add(-shifted).at[sink].add(shifted)
    members = jnp.searchsorted(jnp.cumsum(sizes), jnp.arange(rows * top), side="right").astype(jnp.int32)
    table = members.reshape(top, rows).T
    table = table[jax.random.permutation(jax.random.fold_in(own, 1), rows)]
    offset_by = jax.random.randint(jax.random.fold_in(own, 2), (rows, 1), 0, top)
    return jnp.take_along_axis(table, (jnp.arange(top)[None, :] + offset_by) % top, axis=1)


def shares(count, total, most, skew, full):
    loads = [(1 << 20) // math.isqrt(standing ** skew) + 1 for standing in range(1, count + 1)]
    largest = most if full else min(most, max(-(-total // count), total * loads[0] // sum(loads)))
    least = 1 if total - largest >= count - 1 else 0
    holding, spare = [largest] + [least] * (count - 1), total - largest - least * (count - 1)
    while spare > 0:
        free = [i for i in range(1, count) if holding[i] < largest] or [i for i in range(1, count) if holding[i] < most]
        pool, remaining = sum([loads[i] for i in free]), spare
        for i in free:
            more = min(most - holding[i], max(1, remaining * loads[i] // pool), spare)
            holding[i] = holding[i] + more
            spare = spare - more
    return np.array(holding)


def scatter_about(key, extent, spread, reach, shards=(), kind=jnp.bfloat16):
    entries = spread * jax.random.normal(key, extent, jnp.float32)
    if shards:
        entries = entries * block_scale(key, extent, shards, -0.22, 0.18)
    return jnp.clip(entries, -reach, reach).astype(kind)


def setup_inputs(seed: int = 0) -> dict:
    key_of = jax.random.split(jax.random.key(seed), 9)
    adjoint = scatter_about(key_of[0], (PAIRS, 9, LAGS), 0.05, 0.29882812, ((0, 32),))
    first_block_keys = jax.random.split(jax.random.fold_in(key_of[1], 1), PAIRS // ROWS)
    first_block_turns = jax.random.permutation(jax.random.fold_in(key_of[1], 3), PAIRS // ROWS)
    first_block = jax.vmap(lambda own, number: routed_block(jax.random.fold_in(key_of[1], 2), own, number, ROWS, BLOCKS, 1, CAPACITY, 2))(first_block_keys, first_block_turns).reshape((PAIRS, 1))
    second_station = with_ends(jax.random.randint(key_of[2], (PAIRS,), 0, STATIONS), jax.random.fold_in(key_of[2], 1), 0, STATIONS - 1).astype(jnp.int32)
    station_block = with_ends(jax.random.randint(key_of[3], (STATIONS,), 0, BLOCKS), jax.random.fold_in(key_of[3], 1), 0, BLOCKS - 1).astype(jnp.int32)
    lag_lo = with_ends(jax.random.randint(key_of[4], (PAIRS,), 0, LAGS // 2), jax.random.fold_in(key_of[4], 1), 0, (LAGS // 2) - 1).astype(jnp.int32)
    lag_hi = with_ends(jax.random.randint(key_of[5], (PAIRS,), LAGS // 2 + 1, LAGS + 1), jax.random.fold_in(key_of[5], 1), LAGS // 2 + 1, LAGS).astype(jnp.int32)
    pair_count = ragged_sizes(key_of[6], N_PAIR * N_GRID, 3 * ROWS * N_PAIR * N_GRID // 4, ROWS, 2).astype(jnp.int32)
    green_function = draw_green_function(jax.random.fold_in(key_of[8], 71), 0)
    return {"adjoint": adjoint, "first_block": first_block, "second_station": second_station, "station_block": station_block, "lag_lo": lag_lo, "lag_hi": lag_hi, "pair_count": pair_count, "green_function": green_function}


def dft_table(lag_count, freq_count, band_width):
    offsets = jnp.arange(lag_count, dtype=jnp.int32) - lag_count // 2
    indices = jnp.arange(freq_count, dtype=jnp.int32)
    freq_bins = 24 + indices + 64 * (indices // band_width)
    phases = jnp.mod(offsets[:, None] * freq_bins[None, :], lag_count).astype(jnp.float32) * (2.0 * math.pi / lag_count)
    return jnp.concatenate([jnp.cos(phases), -jnp.sin(phases)], axis=1).astype(jnp.bfloat16)


def reference(adjoint, first_block, second_station, station_block, lag_lo, lag_hi, pair_count, green_function):
    freq_count = BANDS * NF
    phase_table = dft_table(LAGS, freq_count, NF)
    lag_index = jnp.arange(LAGS, dtype=jnp.int32)
    second_ids = station_block[second_station]
    pair_code = (first_block[:, 0] * BLOCKS + second_ids).astype(jnp.int32)
    device_blocks = PAIRS // ROWS

    def accumulate(carry, index):
        start = (index * ROWS).astype(jnp.int32)
        signal = lax.dynamic_slice_in_dim(adjoint, start, ROWS, 0)
        lower = lax.dynamic_slice_in_dim(lag_lo, start, ROWS, 0)
        upper = lax.dynamic_slice_in_dim(lag_hi, start, ROWS, 0)
        codes = lax.dynamic_slice_in_dim(pair_code, start, ROWS, 0)
        live_rows = jnp.arange(ROWS, dtype=jnp.int32) < pair_count[index]
        keep_mask = (lag_index[None, :] >= lower[:, None]) & (lag_index[None, :] < upper[:, None]) & live_rows[:, None]
        windowed = jnp.where(keep_mask[:, None, :], signal, jnp.zeros((), signal.dtype))
        spectra = jnp.dot(windowed.reshape(ROWS * 9, LAGS), phase_table, preferred_element_type=jnp.float32)
        spectra = spectra.astype(jnp.bfloat16).reshape(ROWS, 9 * 2 * freq_count).astype(jnp.float32)
        carry = carry + jax.ops.segment_sum(spectra, codes, num_segments=BLOCKS * BLOCKS)
        return carry, None

    initial = jnp.zeros((BLOCKS * BLOCKS, 9 * 2 * freq_count), jnp.float32)
    totals, _ = lax.scan(accumulate, initial, jnp.arange(device_blocks, dtype=jnp.int32))
    coupling = totals.astype(jnp.bfloat16).astype(jnp.float32).reshape(BLOCKS, BLOCKS, 3, 3, 2, freq_count)

    def one_freq(index):
        field = lax.dynamic_index_in_dim(green_function, index, 3, keepdims=False).astype(jnp.float32)
        factor = lax.dynamic_index_in_dim(coupling, index, 5, keepdims=False)
        field_re = field[:, :, 0]
        field_im = field[:, :, 1]
        factor_re = factor[..., 0]
        factor_im = factor[..., 1]
        response_re = jnp.einsum("vbx,uvab->uax", field_re, factor_re) - jnp.einsum("vbx,uvab->uax", field_im, factor_im)
        response_im = jnp.einsum("vbx,uvab->uax", field_re, factor_im) + jnp.einsum("vbx,uvab->uax", field_im, factor_re)
        return jnp.sum(field_re * response_re + field_im * response_im, axis=(0, 1))

    density = lax.map(one_freq, jnp.arange(freq_count, dtype=jnp.int32))
    return density.reshape(BANDS, NF, -1).sum(axis=1)
```

```python
import functools
import math

import jax
import jax.numpy as jnp
from jax import lax
from jax.experimental import pallas as pl
from jax.experimental.pallas import tpu as pltpu
from jax.sharding import PartitionSpec as P

NF = 256
BANDS = 2


def dft_table(lag_count, freq_count, band_width):
    offsets = jnp.arange(lag_count, dtype=jnp.int32) - lag_count // 2
    indices = jnp.arange(freq_count, dtype=jnp.int32)
    freq_bins = 24 + indices + 64 * (indices // band_width)
    phases = jnp.mod(offsets[:, None] * freq_bins[None, :], lag_count).astype(jnp.float32) * (
        2.0 * math.pi / lag_count
    )
    return jnp.concatenate([jnp.cos(phases), -jnp.sin(phases)], axis=1).astype(jnp.bfloat16)


def transform_rows(signal, phase_table):
    lag_count = signal.shape[-1]
    flat = signal.reshape(-1, lag_count)
    result = jnp.dot(flat, phase_table, preferred_element_type=jnp.float32).astype(jnp.bfloat16)
    return result.reshape(signal.shape[:-1] + (phase_table.shape[1],))


def contract(field, factor):
    return jnp.einsum("vbfx,uvabf->uafx", field, factor, preferred_element_type=jnp.float32)


def body(
    adjoint, first_block, second_station, station_block, lag_lo, lag_hi, pair_count, green_function
):
    row_count, comp_count, lag_count = adjoint.shape
    block_count = green_function.shape[0]
    local_freqs = green_function.shape[3]
    pair_devices = lax.axis_size("pair")
    per_owner = block_count // pair_devices
    capacity = max(2, (4 * row_count + 3 * block_count - 1) // (3 * block_count))
    freq_count = BANDS * NF
    owner_slots = per_owner * capacity
    lag_index = jnp.arange(lag_count, dtype=jnp.int32)
    live_rows = jnp.arange(row_count, dtype=jnp.int32) < pair_count[0]
    keep_mask = (
        (lag_index[None, :] >= lag_lo[:, None])
        & (lag_index[None, :] < lag_hi[:, None])
        & live_rows[:, None]
    )
    windowed = jnp.where(keep_mask[:, None, :], adjoint, jnp.zeros((), jnp.bfloat16))
    first_ids = first_block[:, 0]
    station_ids = jnp.arange(station_block.shape[0], dtype=jnp.int32)
    second_ids = jnp.sum(
        jnp.where(second_station[:, None] == station_ids[None, :], station_block[None, :], 0),
        axis=1,
    )
    members = (first_ids[:, None] == jnp.arange(block_count, dtype=jnp.int32)[None, :]).astype(
        jnp.int32
    )
    ranking = jnp.sum((jnp.cumsum(members, axis=0) - 1) * members, axis=1)
    destination = first_ids * capacity + ranking
    slot_ids = jnp.arange(block_count * capacity, dtype=jnp.int32)
    hits = slot_ids[:, None] == destination[None, :]
    dispatch = hits.astype(jnp.bfloat16)
    slot_second = jnp.sum(jnp.where(hits, second_ids[None, :], 0), axis=1)
    slot_second = slot_second.reshape(pair_devices, owner_slots)
    phase_table = dft_table(lag_count, freq_count, NF)
    packed = jnp.dot(dispatch, windowed.reshape(row_count, -1), preferred_element_type=jnp.float32)
    packed = packed.astype(jnp.bfloat16).reshape(pair_devices, owner_slots, comp_count, lag_count)
    arrived = transform_rows(
        lax.all_to_all(packed, "pair", split_axis=0, concat_axis=0, tiled=True), phase_table
    )
    arrived_second = lax.all_to_all(slot_second, "pair", split_axis=0, concat_axis=0, tiled=True)
    slot_block = jnp.arange(owner_slots, dtype=jnp.int32) // capacity
    pair_code = (slot_block[None, :] * block_count + arrived_second).reshape(-1)
    onehot = (
        pair_code[:, None] == jnp.arange(per_owner * block_count, dtype=jnp.int32)[None, :]
    ).astype(jnp.bfloat16)
    flat_spectra = arrived.reshape(pair_code.shape[0], -1)
    partial_value = jnp.einsum(
        "sk,sc->kc", onehot, flat_spectra, preferred_element_type=jnp.float32
    )
    summed = lax.psum(partial_value, "grid")
    coupling = summed.astype(jnp.bfloat16).reshape(
        per_owner, block_count, comp_count, 2, freq_count
    )
    spread = lax.all_to_all(coupling, "pair", split_axis=4, concat_axis=0, tiled=True)
    factors = spread.reshape(block_count, block_count, 3, 3, 2, local_freqs)
    coupling_re = factors[:, :, :, :, 0]
    coupling_im = factors[:, :, :, :, 1]
    green_re = green_function[:, :, 0]
    green_im = green_function[:, :, 1]
    response_re = contract(green_re, coupling_re) - contract(green_im, coupling_im)
    response_im = contract(green_re, coupling_im) + contract(green_im, coupling_re)
    density = jnp.sum(green_re * response_re + green_im * response_im, axis=(0, 1))
    first_freq = lax.axis_index("pair") * local_freqs
    freq_band = (first_freq + jnp.arange(local_freqs, dtype=jnp.int32)) // NF
    selector = freq_band[None, :] == jnp.arange(BANDS, dtype=jnp.int32)[:, None]
    kernel_part = jnp.sum(jnp.where(selector[:, :, None], density[None, :, :], 0.0), axis=1)
    return lax.psum(kernel_part, "pair")


STEP = 32
PAD_ROWS = 16


def twiddles(lag_count, freq_count, band_width, owners):
    per_owner = freq_count // owners
    column = jnp.arange(2 * freq_count, dtype=jnp.int32)[None, :]
    quarter = (column // per_owner) % 2
    index = (column // (2 * per_owner)) * per_owner + column % per_owner
    freq_bin = 24 + index + 64 * (index // band_width)
    coarse_count = -(-lag_count // STEP)
    coarse = STEP * jnp.arange(coarse_count, dtype=jnp.int32)[:, None] - lag_count // 2
    fine = jnp.arange(STEP, dtype=jnp.int32)[:, None]
    turn = 2.0 * math.pi / lag_count
    coarse_phase = jnp.mod(coarse * freq_bin, lag_count).astype(jnp.float32) * turn
    coarse_phase = coarse_phase + quarter.astype(jnp.float32) * (0.5 * math.pi)
    fine_phase = jnp.mod(fine * freq_bin, lag_count).astype(jnp.float32) * turn
    return jnp.cos(coarse_phase), jnp.sin(coarse_phase), jnp.cos(fine_phase), jnp.sin(fine_phase)


def spectra_kernel(
    owners, lo_ref, hi_ref, count_ref, adjoint_ref, ca_ref, sa_ref, cb_ref, sb_ref, out_ref, win, table, spec
):
    rows, comps, lags = adjoint_ref.shape
    padded = win.shape[1]
    width = table.shape[1] // owners
    coarse = ca_ref.shape[0]
    tail = (lags // 128) * 128
    win[:, tail:] = jnp.zeros((win.shape[0], padded - tail), jnp.bfloat16)
    table[coarse * STEP :, :] = jnp.zeros((padded - coarse * STEP, table.shape[1]), jnp.bfloat16)
    for i in range(coarse):
        part = ca_ref[i : i + 1, :] * cb_ref[...] - sa_ref[i : i + 1, :] * sb_ref[...]
        table[i * STEP : (i + 1) * STEP, :] = part.astype(jnp.bfloat16)
    lag = lax.broadcasted_iota(jnp.int32, (comps, lags), 1)
    zero_rows = jnp.zeros((PAD_ROWS - comps, padded), jnp.bfloat16)
    live = count_ref[0]

    def window(p, carry):
        low = lo_ref[p]
        high = jnp.where(p < live, hi_ref[p], 0)
        keep = (lag >= low) & (lag < high)
        kept = jnp.where(keep, adjoint_ref[p].astype(jnp.float32), 0.0).astype(jnp.bfloat16)
        start = pl.multiple_of(p * PAD_ROWS, PAD_ROWS)
        win[pl.ds(start, PAD_ROWS), :lags] = jnp.concatenate([kept, zero_rows[:, :lags]], axis=0)
        return carry

    lax.fori_loop(0, rows, window, 0, unroll=4)
    chunk = 2 * width
    for n in range(table.shape[1] // chunk):
        part = jnp.dot(win[...], table[:, n * chunk : (n + 1) * chunk], preferred_element_type=jnp.float32)
        spec[:, n * chunk : (n + 1) * chunk] = part.astype(jnp.bfloat16)
    for c in range(comps):
        target = lax.broadcasted_iota(jnp.int32, (rows, rows * PAD_ROWS), 0) * PAD_ROWS + c
        source = lax.broadcasted_iota(jnp.int32, (rows, rows * PAD_ROWS), 1)
        select = (target == source).astype(jnp.float32).astype(jnp.bfloat16)
        picked = jnp.dot(select, spec[...], preferred_element_type=jnp.float32).astype(jnp.bfloat16)
        for o in range(owners):
            out_ref[o, :, c * width : (c + 1) * width] = picked[:, o * width : (o + 1) * width]


def spectra_of(adjoint, lag_lo, lag_hi, pair_count, owners):
    rows, comps, lags = adjoint.shape
    tables = twiddles(lags, BANDS * NF, NF, owners)
    padded = -(-lags // 128) * 128
    columns = 2 * BANDS * NF
    smem = pl.BlockSpec(memory_space=pltpu.SMEM)
    vmem = pl.BlockSpec(memory_space=pltpu.VMEM)
    return pl.pallas_call(
        functools.partial(spectra_kernel, owners),
        out_shape=jax.ShapeDtypeStruct((owners, rows, comps * (columns // owners)), jnp.bfloat16),
        in_specs=[smem, smem, smem] + [vmem] * 5,
        out_specs=vmem,
        scratch_shapes=[
            pltpu.VMEM((rows * PAD_ROWS, padded), jnp.bfloat16),
            pltpu.VMEM((padded, columns), jnp.bfloat16),
            pltpu.VMEM((rows * PAD_ROWS, columns), jnp.bfloat16),
        ],
        compiler_params=pltpu.CompilerParams(vmem_limit_bytes=48 * 1024 * 1024),
        name="spectra",
    )(lag_lo, lag_hi, pair_count, adjoint, *tables)


def swap_matrix(n):
    r = lax.broadcasted_iota(jnp.int32, (n * n, n * n), 0)
    s = lax.broadcasted_iota(jnp.int32, (n * n, n * n), 1)
    same = (r // n == s % n) & (r % n == s // n)
    return same.astype(jnp.float32).astype(jnp.bfloat16)


def transpose_green(green_ref, raw, turned, sems, fetch_only=False, start=0):
    pass


def green_copy(green_ref, raw, sems, part):
    return pltpu.make_async_copy(
        green_ref.at[:, :, :, pl.ds(part * 16, 16), :], raw.at[part % 2], sems.at[part % 2]
    )


def turn_green(green_ref, raw, turned, sems):
    swap = swap_matrix(16)
    blocks = green_ref.shape[0]
    freqs, points = green_ref.shape[3], green_ref.shape[4]
    parts = freqs // 16
    for ri in range(2):
        turned[:, 128 * ri + 3 * blocks : 128 * (ri + 1), :] = jnp.zeros(
            (freqs, 128 - 3 * blocks, points), jnp.bfloat16
        )
    for part in range(parts):
        green_copy(green_ref, raw, sems, part).wait()
        slot = part % 2
        for ri in range(2):
            for b in range(3):
                for v in range(0, blocks, 16):
                    block = raw[slot, v : v + 16, b, ri].reshape(256, points)
                    moved = jnp.dot(swap, block, preferred_element_type=jnp.float32)
                    row = 128 * ri + b * blocks + v
                    turned[part * 16 : (part + 1) * 16, row : row + 16, :] = (
                        moved.astype(jnp.bfloat16).reshape(16, 16, points)
                    )
        if part + 2 < parts:
            green_copy(green_ref, raw, sems, part + 2).start()


def couple(code_of, value_ref, blocks, by_lane):
    pairs = value_ref.shape[0]
    eye = (
        lax.broadcasted_iota(jnp.int32, (128, 128), 0) == lax.broadcasted_iota(jnp.int32, (128, 128), 1)
    ).astype(jnp.float32).astype(jnp.bfloat16)
    codes = code_of()
    group = 8
    gap = jnp.zeros((128 - 3 * blocks, 128), jnp.bfloat16)

    def some(i, carry):
        cell = lax.broadcasted_iota(jnp.int32, (group * blocks, pairs), 0) + i * (group * blocks)
        onehot = (cell == codes).astype(jnp.float32).astype(jnp.bfloat16)
        sums = jnp.dot(onehot, value_ref[...], preferred_element_type=jnp.float32).astype(jnp.bfloat16)
        for u in range(group):
            rows = sums[u * blocks : (u + 1) * blocks]
            pieces = []
            for a in range(3):
                for b in range(3):
                    c = 3 * a + b
                    pieces.append(rows[:, c * 128 : (c + 1) * 128])
                pieces.append(gap)
            stacked = jnp.concatenate(pieces, axis=0)
            flipped = lax.dot_general(
                eye, stacked, (((1,), (1,)), ((), ())), preferred_element_type=jnp.float32
            ).astype(jnp.bfloat16)
            for a in range(3):
                by_lane[a * blocks + i * group + u] = flipped[:, a * 128 : (a + 1) * 128]
        return carry

    lax.fori_loop(0, blocks // group, some, 0)


def spread_matrix(by_lane, system):
    swap = swap_matrix(16)
    count = by_lane.shape[0]
    freqs = system.shape[0]
    for ri in range(2):
        for f in range(0, freqs, 16):
            for i in range(0, count, 16):
                block = by_lane[i : i + 16, ri * freqs + f : ri * freqs + f + 16, :].reshape(256, 128)
                moved = jnp.dot(swap, block, preferred_element_type=jnp.float32)
                moved = moved.reshape(16, 16, 128)
                value = moved.astype(jnp.bfloat16)
                if ri == 0:
                    system[f : f + 16, i : i + 16, 0:128] = value
                    system[f : f + 16, count + i : count + i + 16, 128:256] = value
                else:
                    system[f : f + 16, count + i : count + i + 16, 0:128] = value
                    system[f : f + 16, i : i + 16, 128:256] = (-moved).astype(jnp.bfloat16)


def quadratic(system, turned):
    freqs, rows, _ = system.shape
    points = turned.shape[2]
    half = rows // 2

    def one(f, total):
        field = turned[f]
        response = jnp.dot(system[f], field, preferred_element_type=jnp.float32)
        product = (
            response[:half] * field[:half].astype(jnp.float32)
            + response[half:] * field[128 : 128 + half].astype(jnp.float32)
        )
        return total + jnp.sum(product.reshape(half // 8, 8, points), axis=0)

    total = lax.fori_loop(0, freqs, one, jnp.zeros((8, points), jnp.float32), unroll=2)
    return jnp.sum(total, axis=0, keepdims=True)


def density_kernel(code_ref, value_ref, green_ref, out_ref, raw, turned, by_lane, system, sems):
    blocks = green_ref.shape[0]
    for part in range(2):
        green_copy(green_ref, raw, sems, part).start()
    turn_green(green_ref, raw, turned, sems)
    couple(lambda: code_ref[...], value_ref, blocks, by_lane)
    spread_matrix(by_lane, system)
    out_ref[...] = quadratic(system, turned)


def density_of(codes, values, green):
    blocks, _, _, freqs, points = green.shape
    vmem = pl.BlockSpec(memory_space=pltpu.VMEM)
    return pl.pallas_call(
        density_kernel,
        out_shape=jax.ShapeDtypeStruct((1, points), jnp.float32),
        in_specs=[vmem, vmem, pl.BlockSpec(memory_space=pl.ANY)],
        out_specs=vmem,
        scratch_shapes=[
            pltpu.VMEM((2, blocks, 3, 2, 16, points), jnp.bfloat16),
            pltpu.VMEM((freqs, 256, points), jnp.bfloat16),
            pltpu.VMEM((3 * blocks, 128, 128), jnp.bfloat16),
            pltpu.VMEM((freqs, 6 * blocks, 256), jnp.bfloat16),
            pltpu.SemaphoreType.DMA((2,)),
        ],
        compiler_params=pltpu.CompilerParams(vmem_limit_bytes=56 * 1024 * 1024),
        name="density",
    )(codes, values, green)


def fast_body(
    adjoint, first_block, second_station, station_block, lag_lo, lag_hi, pair_count, green_function
):
    blocks = green_function.shape[0]
    owners = lax.axis_size("pair")
    local_freqs = green_function.shape[3]
    station_ids = jnp.arange(station_block.shape[0], dtype=jnp.int32)
    second_ids = jnp.sum(
        jnp.where(second_station[:, None] == station_ids[None, :], station_block[None, :], 0), axis=1
    )
    codes = first_block[:, 0] * blocks + second_ids
    codes = lax.all_gather(codes, ("grid", "pair"), tiled=True)[None, :]
    spectra = spectra_of(adjoint, lag_lo, lag_hi, pair_count, owners)
    arrived = lax.all_to_all(spectra, "pair", split_axis=0, concat_axis=0, tiled=True)
    arrived = arrived.reshape(-1, arrived.shape[-1])
    values = lax.all_gather(arrived, "grid", tiled=True)
    density = density_of(codes, values, green_function)
    band = lax.axis_index("pair") * local_freqs // NF
    selector = jnp.arange(BANDS, dtype=jnp.int32)[:, None] == band
    return lax.psum(jnp.where(selector, density, 0.0), "pair")


def solution(mesh):
    placed = (
        P(("pair", "grid"), None, None),
        P(("pair", "grid"), None),
        P(("pair", "grid")),
        P(),
        P(("pair", "grid")),
        P(("pair", "grid")),
        P(("pair", "grid")),
        P(None, None, None, "pair", "grid"),
    )
    local_freqs = BANDS * NF // mesh.shape["pair"]
    return jax.shard_map(
        fast_body if local_freqs == 64 else body, mesh=mesh, in_specs=placed, out_specs=P(None, "grid"), check_vma=False
    )
```

```python
import functools
import math

import jax
import jax.numpy as jnp
from jax import lax
from jax.experimental import pallas as pl
from jax.experimental.pallas import tpu as pltpu
from jax.sharding import PartitionSpec as P

NF = 256
BANDS = 2


def dft_table(lag_count, freq_count, band_width):
    offsets = jnp.arange(lag_count, dtype=jnp.int32) - lag_count // 2
    indices = jnp.arange(freq_count, dtype=jnp.int32)
    freq_bins = 24 + indices + 64 * (indices // band_width)
    phases = jnp.mod(offsets[:, None] * freq_bins[None, :], lag_count).astype(jnp.float32) * (
        2.0 * math.pi / lag_count
    )
    return jnp.concatenate([jnp.cos(phases), -jnp.sin(phases)], axis=1).astype(jnp.bfloat16)


def transform_rows(signal, phase_table):
    lag_count = signal.shape[-1]
    flat = signal.reshape(-1, lag_count)
    result = jnp.dot(flat, phase_table, preferred_element_type=jnp.float32).astype(jnp.bfloat16)
    return result.reshape(signal.shape[:-1] + (phase_table.shape[1],))


def contract(field, factor):
    return jnp.einsum("vbfx,uvabf->uafx", field, factor, preferred_element_type=jnp.float32)


def body(
    adjoint, first_block, second_station, station_block, lag_lo, lag_hi, pair_count, green_function
):
    row_count, comp_count, lag_count = adjoint.shape
    block_count = green_function.shape[0]
    local_freqs = green_function.shape[3]
    pair_devices = lax.axis_size("pair")
    per_owner = block_count // pair_devices
    capacity = max(2, (4 * row_count + 3 * block_count - 1) // (3 * block_count))
    freq_count = BANDS * NF
    owner_slots = per_owner * capacity
    lag_index = jnp.arange(lag_count, dtype=jnp.int32)
    live_rows = jnp.arange(row_count, dtype=jnp.int32) < pair_count[0]
    keep_mask = (
        (lag_index[None, :] >= lag_lo[:, None])
        & (lag_index[None, :] < lag_hi[:, None])
        & live_rows[:, None]
    )
    windowed = jnp.where(keep_mask[:, None, :], adjoint, jnp.zeros((), jnp.bfloat16))
    first_ids = first_block[:, 0]
    station_ids = jnp.arange(station_block.shape[0], dtype=jnp.int32)
    second_ids = jnp.sum(
        jnp.where(second_station[:, None] == station_ids[None, :], station_block[None, :], 0),
        axis=1,
    )
    members = (first_ids[:, None] == jnp.arange(block_count, dtype=jnp.int32)[None, :]).astype(
        jnp.int32
    )
    ranking = jnp.sum((jnp.cumsum(members, axis=0) - 1) * members, axis=1)
    destination = first_ids * capacity + ranking
    slot_ids = jnp.arange(block_count * capacity, dtype=jnp.int32)
    hits = slot_ids[:, None] == destination[None, :]
    dispatch = hits.astype(jnp.bfloat16)
    slot_second = jnp.sum(jnp.where(hits, second_ids[None, :], 0), axis=1)
    slot_second = slot_second.reshape(pair_devices, owner_slots)
    phase_table = dft_table(lag_count, freq_count, NF)
    packed = jnp.dot(dispatch, windowed.reshape(row_count, -1), preferred_element_type=jnp.float32)
    packed = packed.astype(jnp.bfloat16).reshape(pair_devices, owner_slots, comp_count, lag_count)
    arrived = transform_rows(
        lax.all_to_all(packed, "pair", split_axis=0, concat_axis=0, tiled=True), phase_table
    )
    arrived_second = lax.all_to_all(slot_second, "pair", split_axis=0, concat_axis=0, tiled=True)
    slot_block = jnp.arange(owner_slots, dtype=jnp.int32) // capacity
    pair_code = (slot_block[None, :] * block_count + arrived_second).reshape(-1)
    onehot = (
        pair_code[:, None] == jnp.arange(per_owner * block_count, dtype=jnp.int32)[None, :]
    ).astype(jnp.bfloat16)
    flat_spectra = arrived.reshape(pair_code.shape[0], -1)
    partial_value = jnp.einsum(
        "sk,sc->kc", onehot, flat_spectra, preferred_element_type=jnp.float32
    )
    summed = lax.psum(partial_value, "grid")
    coupling = summed.astype(jnp.bfloat16).reshape(
        per_owner, block_count, comp_count, 2, freq_count
    )
    spread = lax.all_to_all(coupling, "pair", split_axis=4, concat_axis=0, tiled=True)
    factors = spread.reshape(block_count, block_count, 3, 3, 2, local_freqs)
    coupling_re = factors[:, :, :, :, 0]
    coupling_im = factors[:, :, :, :, 1]
    green_re = green_function[:, :, 0]
    green_im = green_function[:, :, 1]
    response_re = contract(green_re, coupling_re) - contract(green_im, coupling_im)
    response_im = contract(green_re, coupling_im) + contract(green_im, coupling_re)
    density = jnp.sum(green_re * response_re + green_im * response_im, axis=(0, 1))
    first_freq = lax.axis_index("pair") * local_freqs
    freq_band = (first_freq + jnp.arange(local_freqs, dtype=jnp.int32)) // NF
    selector = freq_band[None, :] == jnp.arange(BANDS, dtype=jnp.int32)[:, None]
    kernel_part = jnp.sum(jnp.where(selector[:, :, None], density[None, :, :], 0.0), axis=1)
    return lax.psum(kernel_part, "pair")


STEP = 32


def twiddles(lag_count, freq_count, band_width, owners):
    per_owner = freq_count // owners
    column = jnp.arange(2 * freq_count, dtype=jnp.int32)[None, :]
    quarter = (column // per_owner) % 2
    index = (column // (2 * per_owner)) * per_owner + column % per_owner
    freq_bin = 24 + index + 64 * (index // band_width)
    coarse_count = -(-lag_count // STEP)
    coarse = STEP * jnp.arange(coarse_count, dtype=jnp.int32)[:, None] - lag_count // 2
    fine = jnp.arange(STEP, dtype=jnp.int32)[:, None]
    turn = 2.0 * math.pi / lag_count
    coarse_phase = jnp.mod(coarse * freq_bin, lag_count).astype(jnp.float32) * turn
    coarse_phase = coarse_phase + quarter.astype(jnp.float32) * (0.5 * math.pi)
    fine_phase = jnp.mod(fine * freq_bin, lag_count).astype(jnp.float32) * turn
    return jnp.cos(coarse_phase), jnp.sin(coarse_phase), jnp.cos(fine_phase), jnp.sin(fine_phase)


def swap_matrix(n):
    r = lax.broadcasted_iota(jnp.int32, (n * n, n * n), 0)
    s = lax.broadcasted_iota(jnp.int32, (n * n, n * n), 1)
    same = (r // n == s % n) & (r % n == s // n)
    return same.astype(jnp.float32).astype(jnp.bfloat16)


def green_copy(green_ref, raw, sems, part):
    return pltpu.make_async_copy(
        green_ref.at[:, :, :, pl.ds(part * 16, 16), :], raw.at[part % 2], sems.at[part % 2]
    )


def clear_gaps(turned, blocks):
    freqs, _, points = turned.shape
    for ri in range(2):
        turned[:, 128 * ri + 3 * blocks : 128 * (ri + 1), :] = jnp.zeros(
            (freqs, 128 - 3 * blocks, points), jnp.bfloat16
        )


def turn_green(green_ref, raw, turned, sems, swap, part, ri):
    blocks, points = green_ref.shape[0], green_ref.shape[4]
    slot = part % 2
    if ri == 0:
        green_copy(green_ref, raw, sems, part).wait()
    for b in range(3):
        for v in range(0, blocks, 16):
            block = raw[slot, v : v + 16, b, ri].reshape(256, points)
            moved = jnp.dot(swap, block, preferred_element_type=jnp.float32)
            row = 128 * ri + b * blocks + v
            turned[part * 16 : (part + 1) * 16, row : row + 16, :] = (
                moved.astype(jnp.bfloat16).reshape(16, 16, points)
            )
    if ri == 1 and part + 2 < green_ref.shape[3] // 16:
        green_copy(green_ref, raw, sems, part + 2).start()


def couple(codes, value_ref, blocks, by_lane):
    pairs = value_ref.shape[0] * value_ref.shape[1]
    eye = (
        lax.broadcasted_iota(jnp.int32, (128, 128), 0) == lax.broadcasted_iota(jnp.int32, (128, 128), 1)
    ).astype(jnp.float32).astype(jnp.bfloat16)
    group = 8
    gap = jnp.zeros((128 - 3 * blocks, 128), jnp.bfloat16)

    def some(i, carry):
        cell = lax.broadcasted_iota(jnp.int32, (group * blocks, pairs), 0) + i * (group * blocks)
        onehot = (cell == codes).astype(jnp.float32).astype(jnp.bfloat16)
        values = value_ref[...].reshape(pairs, value_ref.shape[2])
        sums = jnp.dot(onehot, values, preferred_element_type=jnp.float32).astype(jnp.bfloat16)
        for u in range(group):
            rows = sums[u * blocks : (u + 1) * blocks]
            pieces = []
            for a in range(3):
                for b in range(3):
                    c = 3 * a + b
                    pieces.append(rows[:, c * 128 : (c + 1) * 128])
                pieces.append(gap)
            stacked = jnp.concatenate(pieces, axis=0)
            flipped = lax.dot_general(
                eye, stacked, (((1,), (1,)), ((), ())), preferred_element_type=jnp.float32
            ).astype(jnp.bfloat16)
            for a in range(3):
                by_lane[a * blocks + i * group + u] = flipped[:, a * 128 : (a + 1) * 128]
        return carry

    lax.fori_loop(0, blocks // group, some, 0)


def spread_matrix(by_lane, system):
    swap = swap_matrix(16)
    count = by_lane.shape[0]
    freqs = system.shape[0]
    for ri in range(2):
        for f in range(0, freqs, 16):
            for i in range(0, count, 16):
                block = by_lane[i : i + 16, ri * freqs + f : ri * freqs + f + 16, :].reshape(256, 128)
                moved = jnp.dot(swap, block, preferred_element_type=jnp.float32)
                moved = moved.reshape(16, 16, 128)
                value = moved.astype(jnp.bfloat16)
                if ri == 0:
                    system[f : f + 16, i : i + 16, 0:128] = value
                    system[f : f + 16, count + i : count + i + 16, 128:256] = value
                else:
                    system[f : f + 16, count + i : count + i + 16, 0:128] = value
                    system[f : f + 16, i : i + 16, 128:256] = (-moved).astype(jnp.bfloat16)


def quadratic(system, turned):
    freqs, rows, _ = system.shape
    points = turned.shape[2]
    half = rows // 2

    def one(f, total):
        field = turned[f]
        response = jnp.dot(system[f], field, preferred_element_type=jnp.float32)
        product = (
            response[:half] * field[:half].astype(jnp.float32)
            + response[half:] * field[128 : 128 + half].astype(jnp.float32)
        )
        return total + jnp.sum(product.reshape(half // 8, 8, points), axis=0)

    total = lax.fori_loop(0, freqs, one, jnp.zeros((8, points), jnp.float32), unroll=2)
    return jnp.sum(total, axis=0, keepdims=True)


def make_table(table, ca_ref, sa_ref, cb_ref, sb_ref):
    coarse = ca_ref.shape[0]
    table[coarse * STEP :, :] = jnp.zeros((table.shape[0] - coarse * STEP, table.shape[1]), jnp.bfloat16)
    for i in range(coarse):
        part = ca_ref[i : i + 1, :] * cb_ref[...] - sa_ref[i : i + 1, :] * sb_ref[...]
        table[i * STEP : (i + 1) * STEP, :] = part.astype(jnp.bfloat16)


def make_window(win, adjoint_ref, lo_ref, hi_ref):
    comps, rows, lags = adjoint_ref.shape
    tail = (lags // 128) * 128
    win[:, tail:] = jnp.zeros((win.shape[0], win.shape[1] - tail), jnp.bfloat16)
    lag = lax.broadcasted_iota(jnp.int32, (rows, lags), 1)
    keep = (lag >= lo_ref[...]) & (lag < hi_ref[...])
    for c in range(comps):
        kept = jnp.where(keep, adjoint_ref[c].astype(jnp.float32), 0.0)
        win[c * rows : (c + 1) * rows, :lags] = kept.astype(jnp.bfloat16)


def main_kernel(
    owners,
    adjoint_ref,
    lo_ref,
    hi_ref,
    code_ref,
    ca_ref,
    sa_ref,
    cb_ref,
    sb_ref,
    green_ref,
    out_ref,
    win,
    table,
    outbox,
    values,
    codes,
    raw,
    turned,
    by_lane,
    system,
    parts,
    green_sems,
    own_sems,
    send_pair,
    recv_pair,
    send_chip,
    recv_chip,
    send_core,
    recv_core,
    send_part,
    recv_part,
):
    comps, rows, _ = adjoint_ref.shape
    blocks, freqs = green_ref.shape[0], green_ref.shape[3]
    pair, grid = lax.axis_index("pair"), lax.axis_index("grid")
    other_chip = lax.rem(grid + 2, 4)
    other_core = grid + 1 - 2 * lax.rem(grid, 2)
    barrier = pltpu.get_barrier_semaphore()

    def greet(p, g):
        pl.semaphore_signal(barrier, inc=1, device_id=(p, g), device_id_type=pl.DeviceIdType.MESH)

    for k in range(1, owners):
        greet(lax.rem(pair + k, owners), grid)
    greet(pair, other_chip)
    greet(pair, other_core)
    for part in range(2):
        green_copy(green_ref, raw, green_sems, part).start()
    make_table(table, ca_ref, sa_ref, cb_ref, sb_ref)
    make_window(win, adjoint_ref, lo_ref, hi_ref)
    pl.semaphore_wait(barrier, owners + 1)

    width = 2 * freqs
    couples = owners // 2
    z, y = pair // 2, lax.rem(pair, 2)
    mine = grid * owners + pair

    def remote(src, dst, send, recv, p, g):
        return pltpu.make_async_remote_copy(
            src_ref=src, dst_ref=dst, send_sem=send, recv_sem=recv,
            device_id=(p, g), device_id_type=pl.DeviceIdType.MESH,
        )

    def to_owner(o):
        return (
            remote(outbox.at[o], values.at[mine], send_pair.at[0, o], recv_pair.at[0, pair], o, grid),
            remote(code_ref, codes.at[mine], send_pair.at[1, o], recv_pair.at[1, pair], o, grid),
        )

    def from_source(q):
        slot = grid * owners + q
        return (
            remote(outbox.at[q], values.at[slot], send_pair.at[0, q], recv_pair.at[0, q], q, grid),
            remote(code_ref, codes.at[slot], send_pair.at[1, q], recv_pair.at[1, q], q, grid),
        )

    def between_chips(q, from_grid):
        slot = from_grid * owners + q
        return tuple(
            remote(ref.at[slot], ref.at[slot], send_chip.at[i, q], recv_chip.at[i, q], pair, other_chip)
            for i, ref in enumerate((values, codes))
        )

    def between_cores(q, from_grid, turn):
        slot = from_grid * owners + q
        return tuple(
            remote(
                ref.at[slot], ref.at[slot], send_core.at[i, turn, q], recv_core.at[i, turn, q],
                pair, other_core,
            )
            for i, ref in enumerate((values, codes))
        )

    order = [0] + [couples // 2] + [k for k in range(1, couples) if k != couples // 2]
    for k in order:
        zz = lax.rem(z + k, couples)
        start = pl.multiple_of(zz * 2 * width, 2 * width)
        spectra = jnp.dot(
            win[...], table[:, pl.ds(start, 2 * width)], preferred_element_type=jnp.float32
        ).astype(jnp.bfloat16)
        for h in range(2):
            for c in range(comps):
                outbox[2 * zz + h, :, c * width : (c + 1) * width] = spectra[
                    c * rows : (c + 1) * rows, h * width : (h + 1) * width
                ]
        if k == 0:
            own = (
                pltpu.make_async_copy(outbox.at[pair], values.at[mine], own_sems.at[0]),
                pltpu.make_async_copy(code_ref, codes.at[mine], own_sems.at[1]),
            )
            for copy in own:
                copy.start()
            for copy in to_owner(2 * z + 1 - y):
                copy.start()
            for copy in own:
                copy.wait()
            for copy in between_chips(pair, grid) + between_cores(pair, grid, 0):
                copy.start()
        else:
            for h in range(2):
                for copy in to_owner(2 * zz + h):
                    copy.start()

    sources = [pair, 2 * z + 1 - y]
    for k in order[1:]:
        back = lax.rem(z + couples - k, couples)
        sources += [2 * back, 2 * back + 1]
    swap = swap_matrix(16)
    clear_gaps(turned, blocks)
    green_steps = [(part, ri) for part in range(freqs // 16) for ri in range(2)]
    for step, q in enumerate(sources):
        turn_green(green_ref, raw, turned, green_sems, swap, *green_steps[step])
        if step > 0:
            for copy in from_source(q):
                copy.wait_recv()
            for copy in between_chips(q, grid) + between_cores(q, grid, 0):
                copy.start()
            before = sources[step - 1]
            for copy in between_chips(before, grid):
                copy.wait_recv()
            for copy in between_cores(before, other_chip, 1):
                copy.start()
    last = sources[-1]
    for copy in between_chips(last, grid):
        copy.wait_recv()
    for copy in between_cores(last, other_chip, 1):
        copy.start()
    for q in sources:
        for copy in between_cores(q, grid, 0) + between_cores(q, other_chip, 1):
            copy.wait_recv()

    code_row = jnp.concatenate([codes[i][0:1, 0:rows] for i in range(codes.shape[0])], axis=1)
    couple(code_row, values, blocks, by_lane)
    spread_matrix(by_lane, system)
    parts[pair] = quadratic(system, turned)

    def to_peer(k):
        there = lax.rem(pair + k, owners)
        return remote(parts.at[pair], parts.at[pair], send_part.at[there], recv_part.at[pair], there, grid)

    def from_peer(k):
        there = lax.rem(pair + k, owners)
        return remote(parts.at[there], parts.at[there], send_part.at[there], recv_part.at[there], there, grid)

    for k in range(1, owners):
        to_peer(k).start()
    for k in range(1, owners):
        from_peer(k).wait_recv()
    for band in range(BANDS):
        members = [parts[o] for o in range(owners) if o * freqs // NF == band]
        out_ref[band : band + 1, :] = sum(members[1:], members[0])
    for q in sources:
        for copy in between_chips(q, grid) + between_cores(q, grid, 0) + between_cores(q, other_chip, 1):
            copy.wait_send()
    for q in sources[1:]:
        for copy in to_owner(q):
            copy.wait_send()
    for k in range(1, owners):
        to_peer(k).wait_send()


def fast_body(
    adjoint, first_block, second_station, station_block, lag_lo, lag_hi, pair_count, green_function
):
    rows, comps, lags = adjoint.shape
    blocks, _, _, freqs, points = green_function.shape
    owners, grids = lax.axis_size("pair"), lax.axis_size("grid")
    station_ids = jnp.arange(station_block.shape[0], dtype=jnp.int32)
    second_ids = jnp.sum(
        jnp.where(second_station[:, None] == station_ids[None, :], station_block[None, :], 0), axis=1
    )
    code = first_block[:, 0] * blocks + second_ids
    code = jnp.broadcast_to(jnp.pad(code, (0, 128 - rows))[None, :], (8, 128))
    live = jnp.arange(rows, dtype=jnp.int32) < pair_count[0]
    high = jnp.where(live, lag_hi, 0)[:, None]
    tables = twiddles(lags, BANDS * NF, NF, owners)
    padded = -(-lags // 128) * 128
    columns = 2 * BANDS * NF
    chunks = owners * grids
    vmem = pl.BlockSpec(memory_space=pltpu.VMEM)
    dma = pltpu.SemaphoreType.DMA
    return pl.pallas_call(
        functools.partial(main_kernel, owners),
        out_shape=jax.ShapeDtypeStruct((BANDS, points), jnp.float32),
        in_specs=[vmem] * 8 + [pl.BlockSpec(memory_space=pl.ANY)],
        out_specs=vmem,
        scratch_shapes=[
            pltpu.VMEM((rows * comps, padded), jnp.bfloat16),
            pltpu.VMEM((padded, columns), jnp.bfloat16),
            pltpu.VMEM((owners, rows, comps * 2 * freqs), jnp.bfloat16),
            pltpu.VMEM((chunks, rows, comps * 2 * freqs), jnp.bfloat16),
            pltpu.VMEM((chunks, 8, 128), jnp.int32),
            pltpu.VMEM((2, blocks, 3, 2, 16, points), jnp.bfloat16),
            pltpu.VMEM((freqs, 256, points), jnp.bfloat16),
            pltpu.VMEM((3 * blocks, 128, 128), jnp.bfloat16),
            pltpu.VMEM((freqs, 6 * blocks, 256), jnp.bfloat16),
            pltpu.VMEM((owners, 1, points), jnp.float32),
            dma((2,)),
            dma((2,)),
            dma((2, owners)),
            dma((2, owners)),
            dma((2, owners)),
            dma((2, owners)),
            dma((2, 2, owners)),
            dma((2, 2, owners)),
            dma((owners,)),
            dma((owners,)),
        ],
        compiler_params=pltpu.CompilerParams(
            collective_id=0, has_side_effects=True, vmem_limit_bytes=60 * 1024 * 1024
        ),
        name="sensitivity",
    )(jnp.transpose(adjoint, (1, 0, 2)), lag_lo[:, None], high, code, *tables, green_function)


def solution(mesh):
    placed = (
        P(("pair", "grid"), None, None),
        P(("pair", "grid"), None),
        P(("pair", "grid")),
        P(),
        P(("pair", "grid")),
        P(("pair", "grid")),
        P(("pair", "grid")),
        P(None, None, None, "pair", "grid"),
    )
    local_freqs = BANDS * NF // mesh.shape["pair"]
    return jax.shard_map(
        fast_body if local_freqs == 64 else body, mesh=mesh, in_specs=placed, out_specs=P(None, "grid"), check_vma=False
    )
```

```python
import functools
import math

import jax
import jax.numpy as jnp
from jax import lax
from jax.experimental import pallas as pl
from jax.experimental.pallas import tpu as pltpu
from jax.sharding import PartitionSpec as P

NF = 256
BANDS = 2


def dft_table(lag_count, freq_count, band_width):
    offsets = jnp.arange(lag_count, dtype=jnp.int32) - lag_count // 2
    indices = jnp.arange(freq_count, dtype=jnp.int32)
    freq_bins = 24 + indices + 64 * (indices // band_width)
    phases = jnp.mod(offsets[:, None] * freq_bins[None, :], lag_count).astype(jnp.float32) * (
        2.0 * math.pi / lag_count
    )
    return jnp.concatenate([jnp.cos(phases), -jnp.sin(phases)], axis=1).astype(jnp.bfloat16)


def transform_rows(signal, phase_table):
    lag_count = signal.shape[-1]
    flat = signal.reshape(-1, lag_count)
    result = jnp.dot(flat, phase_table, preferred_element_type=jnp.float32).astype(jnp.bfloat16)
    return result.reshape(signal.shape[:-1] + (phase_table.shape[1],))


def contract(field, factor):
    return jnp.einsum("vbfx,uvabf->uafx", field, factor, preferred_element_type=jnp.float32)


def body(
    adjoint, first_block, second_station, station_block, lag_lo, lag_hi, pair_count, green_function
):
    row_count, comp_count, lag_count = adjoint.shape
    block_count = green_function.shape[0]
    local_freqs = green_function.shape[3]
    pair_devices = lax.axis_size("pair")
    per_owner = block_count // pair_devices
    capacity = max(2, (4 * row_count + 3 * block_count - 1) // (3 * block_count))
    freq_count = BANDS * NF
    owner_slots = per_owner * capacity
    lag_index = jnp.arange(lag_count, dtype=jnp.int32)
    live_rows = jnp.arange(row_count, dtype=jnp.int32) < pair_count[0]
    keep_mask = (
        (lag_index[None, :] >= lag_lo[:, None])
        & (lag_index[None, :] < lag_hi[:, None])
        & live_rows[:, None]
    )
    windowed = jnp.where(keep_mask[:, None, :], adjoint, jnp.zeros((), jnp.bfloat16))
    first_ids = first_block[:, 0]
    station_ids = jnp.arange(station_block.shape[0], dtype=jnp.int32)
    second_ids = jnp.sum(
        jnp.where(second_station[:, None] == station_ids[None, :], station_block[None, :], 0),
        axis=1,
    )
    members = (first_ids[:, None] == jnp.arange(block_count, dtype=jnp.int32)[None, :]).astype(
        jnp.int32
    )
    ranking = jnp.sum((jnp.cumsum(members, axis=0) - 1) * members, axis=1)
    destination = first_ids * capacity + ranking
    slot_ids = jnp.arange(block_count * capacity, dtype=jnp.int32)
    hits = slot_ids[:, None] == destination[None, :]
    dispatch = hits.astype(jnp.bfloat16)
    slot_second = jnp.sum(jnp.where(hits, second_ids[None, :], 0), axis=1)
    slot_second = slot_second.reshape(pair_devices, owner_slots)
    phase_table = dft_table(lag_count, freq_count, NF)
    packed = jnp.dot(dispatch, windowed.reshape(row_count, -1), preferred_element_type=jnp.float32)
    packed = packed.astype(jnp.bfloat16).reshape(pair_devices, owner_slots, comp_count, lag_count)
    arrived = transform_rows(
        lax.all_to_all(packed, "pair", split_axis=0, concat_axis=0, tiled=True), phase_table
    )
    arrived_second = lax.all_to_all(slot_second, "pair", split_axis=0, concat_axis=0, tiled=True)
    slot_block = jnp.arange(owner_slots, dtype=jnp.int32) // capacity
    pair_code = (slot_block[None, :] * block_count + arrived_second).reshape(-1)
    onehot = (
        pair_code[:, None] == jnp.arange(per_owner * block_count, dtype=jnp.int32)[None, :]
    ).astype(jnp.bfloat16)
    flat_spectra = arrived.reshape(pair_code.shape[0], -1)
    partial_value = jnp.einsum(
        "sk,sc->kc", onehot, flat_spectra, preferred_element_type=jnp.float32
    )
    summed = lax.psum(partial_value, "grid")
    coupling = summed.astype(jnp.bfloat16).reshape(
        per_owner, block_count, comp_count, 2, freq_count
    )
    spread = lax.all_to_all(coupling, "pair", split_axis=4, concat_axis=0, tiled=True)
    factors = spread.reshape(block_count, block_count, 3, 3, 2, local_freqs)
    coupling_re = factors[:, :, :, :, 0]
    coupling_im = factors[:, :, :, :, 1]
    green_re = green_function[:, :, 0]
    green_im = green_function[:, :, 1]
    response_re = contract(green_re, coupling_re) - contract(green_im, coupling_im)
    response_im = contract(green_re, coupling_im) + contract(green_im, coupling_re)
    density = jnp.sum(green_re * response_re + green_im * response_im, axis=(0, 1))
    first_freq = lax.axis_index("pair") * local_freqs
    freq_band = (first_freq + jnp.arange(local_freqs, dtype=jnp.int32)) // NF
    selector = freq_band[None, :] == jnp.arange(BANDS, dtype=jnp.int32)[:, None]
    kernel_part = jnp.sum(jnp.where(selector[:, :, None], density[None, :, :], 0.0), axis=1)
    return lax.psum(kernel_part, "pair")


STEP = 32


def twiddles(lag_count, freq_count, band_width, owners):
    per_owner = freq_count // owners
    column = jnp.arange(2 * freq_count, dtype=jnp.int32)[None, :]
    quarter = (column // per_owner) % 2
    index = (column // (2 * per_owner)) * per_owner + column % per_owner
    freq_bin = 24 + index + 64 * (index // band_width)
    row = jnp.arange(16 + STEP, dtype=jnp.int32)[:, None]
    offset = jnp.where(
        row < 8, 8 * STEP * row - lag_count // 2, jnp.where(row < 16, STEP * (row - 8), row - 16)
    )
    phase = jnp.mod(offset * freq_bin, lag_count).astype(jnp.float32) * (2.0 * math.pi / lag_count)
    phase = phase + jnp.where(row < 8, quarter, 0).astype(jnp.float32) * (0.5 * math.pi)
    return jnp.cos(phase), jnp.sin(phase)


def swap_matrix(n):
    r = lax.broadcasted_iota(jnp.int32, (n * n, n * n), 0)
    s = lax.broadcasted_iota(jnp.int32, (n * n, n * n), 1)
    same = (r // n == s % n) & (r % n == s // n)
    return same.astype(jnp.float32).astype(jnp.bfloat16)


def green_copy(green_ref, raw, sems, part):
    return pltpu.make_async_copy(
        green_ref.at[:, :, :, pl.ds(part * 16, 16), :], raw.at[part % 2], sems.at[part % 2]
    )


def clear_gaps(turned, blocks):
    freqs, _, points = turned.shape
    for ri in range(2):
        turned[:, 128 * ri + 3 * blocks : 128 * (ri + 1), :] = jnp.zeros(
            (freqs, 128 - 3 * blocks, points), jnp.bfloat16
        )


def turn_green(green_ref, raw, turned, sems, swap, part, ri):
    blocks, points = green_ref.shape[0], green_ref.shape[4]
    slot = part % 2
    if ri == 0:
        green_copy(green_ref, raw, sems, part).wait()
    for b in range(3):
        for v in range(0, blocks, 16):
            block = raw[slot, v : v + 16, b, ri].reshape(256, points)
            moved = jnp.dot(swap, block, preferred_element_type=jnp.float32)
            row = 128 * ri + b * blocks + v
            turned[part * 16 : (part + 1) * 16, row : row + 16, :] = (
                moved.astype(jnp.bfloat16).reshape(16, 16, points)
            )
    if ri == 1 and part + 2 < green_ref.shape[3] // 16:
        green_copy(green_ref, raw, sems, part + 2).start()


def couple(codes, value_ref, blocks, by_lane):
    pairs = value_ref.shape[0] * value_ref.shape[1]
    eye = (
        lax.broadcasted_iota(jnp.int32, (128, 128), 0) == lax.broadcasted_iota(jnp.int32, (128, 128), 1)
    ).astype(jnp.float32).astype(jnp.bfloat16)
    group = 8
    gap = jnp.zeros((128 - 3 * blocks, 128), jnp.bfloat16)

    def some(i, carry):
        cell = lax.broadcasted_iota(jnp.int32, (group * blocks, pairs), 0) + i * (group * blocks)
        onehot = (cell == codes).astype(jnp.float32).astype(jnp.bfloat16)
        values = value_ref[...].reshape(pairs, value_ref.shape[2])
        sums = jnp.dot(onehot, values, preferred_element_type=jnp.float32).astype(jnp.bfloat16)
        for u in range(group):
            rows = sums[u * blocks : (u + 1) * blocks]
            pieces = []
            for a in range(3):
                for b in range(3):
                    c = 3 * a + b
                    pieces.append(rows[:, c * 128 : (c + 1) * 128])
                pieces.append(gap)
            stacked = jnp.concatenate(pieces, axis=0)
            flipped = lax.dot_general(
                eye, stacked, (((1,), (1,)), ((), ())), preferred_element_type=jnp.float32
            ).astype(jnp.bfloat16)
            for a in range(3):
                by_lane[a * blocks + i * group + u] = flipped[:, a * 128 : (a + 1) * 128]
        return carry

    lax.fori_loop(0, blocks // group, some, 0)


def spread_matrix(by_lane, system):
    swap = swap_matrix(16)
    count = by_lane.shape[0]
    freqs = system.shape[0]
    for ri in range(2):
        for f in range(0, freqs, 16):
            for i in range(0, count, 16):
                block = by_lane[i : i + 16, ri * freqs + f : ri * freqs + f + 16, :].reshape(256, 128)
                moved = jnp.dot(swap, block, preferred_element_type=jnp.float32)
                moved = moved.reshape(16, 16, 128)
                value = moved.astype(jnp.bfloat16)
                if ri == 0:
                    system[f : f + 16, i : i + 16, 0:128] = value
                    system[f : f + 16, count + i : count + i + 16, 128:256] = value
                else:
                    system[f : f + 16, count + i : count + i + 16, 0:128] = value
                    system[f : f + 16, i : i + 16, 128:256] = (-moved).astype(jnp.bfloat16)


def quadratic(system, turned):
    freqs, rows, _ = system.shape
    points = turned.shape[2]
    half = rows // 2

    def one(f, total):
        field = turned[f]
        response = jnp.dot(system[f], field, preferred_element_type=jnp.float32)
        product = (
            response[:half] * field[:half].astype(jnp.float32)
            + response[half:] * field[128 : 128 + half].astype(jnp.float32)
        )
        return total + jnp.sum(product.reshape(half // 8, 8, points), axis=0)

    total = lax.fori_loop(0, freqs, one, jnp.zeros((8, points), jnp.float32), unroll=4)
    return jnp.sum(total, axis=0, keepdims=True)


def make_table(table, cos_ref, sin_ref):
    cos_mid, sin_mid = cos_ref[8:16, :], sin_ref[8:16, :]
    cos_fine, sin_fine = cos_ref[16:, :], sin_ref[16:, :]
    for i in range(table.shape[0] // (8 * STEP)):
        cos_top, sin_top = cos_ref[i : i + 1, :], sin_ref[i : i + 1, :]
        cos_part = cos_top * cos_mid - sin_top * sin_mid
        sin_part = sin_top * cos_mid + cos_top * sin_mid
        for j in range(8):
            part = cos_part[j : j + 1] * cos_fine - sin_part[j : j + 1] * sin_fine
            row = (8 * i + j) * STEP
            table[row : row + STEP, :] = part.astype(jnp.bfloat16)


def to_column(row):
    n = row.shape[1]
    same = lax.broadcasted_iota(jnp.int32, (n, n), 0) == lax.broadcasted_iota(jnp.int32, (n, n), 1)
    return jnp.sum(jnp.where(same, row.astype(jnp.float32), 0.0), axis=1, keepdims=True)


def to_row(column):
    n = column.shape[0]
    same = lax.broadcasted_iota(jnp.int32, (n, n), 0) == lax.broadcasted_iota(jnp.int32, (n, n), 1)
    return jnp.sum(jnp.where(same, column, 0.0), axis=0, keepdims=True)


def make_codes(code_ref, first_ref, second_ref, station_ref, blocks):
    rows, stations = first_ref.shape[1], station_ref.shape[1]
    second = to_column(second_ref[...]).astype(jnp.int32)
    hit = lax.broadcasted_iota(jnp.int32, (rows, stations), 1) == second
    named = jnp.where(hit, station_ref[...].astype(jnp.float32), 0.0)
    named = to_row(jnp.sum(named, axis=1, keepdims=True)).astype(jnp.int32)
    code_ref[...] = jnp.zeros(code_ref.shape, jnp.int32)
    code_ref[0:1, 0:rows] = first_ref[...] * blocks + named


def make_window(win, adjoint_ref, lo_ref, hi_ref, count_ref):
    comps, rows, lags = adjoint_ref.shape
    live = lax.broadcasted_iota(jnp.int32, (1, rows), 1) < count_ref[...]
    low = to_column(lo_ref[...]).astype(jnp.int32)
    high = to_column(jnp.where(live, hi_ref[...], 0)).astype(jnp.int32)
    tail = (lags // 128) * 128
    win[:, tail:] = jnp.zeros((win.shape[0], win.shape[1] - tail), jnp.bfloat16)
    lag = lax.broadcasted_iota(jnp.int32, (rows, lags), 1)
    keep = (lag >= low) & (lag < high)
    for c in range(comps):
        kept = jnp.where(keep, adjoint_ref[c].astype(jnp.float32), 0.0)
        win[c * rows : (c + 1) * rows, :lags] = kept.astype(jnp.bfloat16)


def main_kernel(
    owners,
    adjoint_ref,
    lo_ref,
    hi_ref,
    count_ref,
    first_ref,
    second_ref,
    station_ref,
    cos_ref,
    sin_ref,
    green_ref,
    out_ref,
    win,
    table,
    code_ref,
    outbox,
    values,
    codes,
    raw,
    turned,
    by_lane,
    system,
    parts,
    green_sems,
    own_sems,
    send_pair,
    recv_pair,
    send_chip,
    recv_chip,
    send_core,
    recv_core,
    send_part,
    recv_part,
):
    comps, rows, _ = adjoint_ref.shape
    blocks, freqs = green_ref.shape[0], green_ref.shape[3]
    pair, grid = lax.axis_index("pair"), lax.axis_index("grid")
    other_chip = lax.rem(grid + 2, 4)
    other_core = grid + 1 - 2 * lax.rem(grid, 2)
    barrier = pltpu.get_barrier_semaphore()

    def greet(p, g):
        pl.semaphore_signal(barrier, inc=1, device_id=(p, g), device_id_type=pl.DeviceIdType.MESH)

    for k in range(1, owners):
        greet(lax.rem(pair + k, owners), grid)
    greet(pair, other_chip)
    greet(pair, other_core)
    for part in range(2):
        green_copy(green_ref, raw, green_sems, part).start()
    make_codes(code_ref, first_ref, second_ref, station_ref, blocks)
    make_table(table, cos_ref, sin_ref)
    make_window(win, adjoint_ref, lo_ref, hi_ref, count_ref)
    pl.semaphore_wait(barrier, owners + 1)

    width = 2 * freqs
    couples = owners // 2
    z, y = pair // 2, lax.rem(pair, 2)
    mine = grid * owners + pair

    def remote(src, dst, send, recv, p, g):
        return pltpu.make_async_remote_copy(
            src_ref=src, dst_ref=dst, send_sem=send, recv_sem=recv,
            device_id=(p, g), device_id_type=pl.DeviceIdType.MESH,
        )

    def to_owner(o):
        return (
            remote(outbox.at[o], values.at[mine], send_pair.at[0, o], recv_pair.at[0, pair], o, grid),
            remote(code_ref, codes.at[mine], send_pair.at[1, o], recv_pair.at[1, pair], o, grid),
        )

    def from_source(q):
        slot = grid * owners + q
        return (
            remote(outbox.at[q], values.at[slot], send_pair.at[0, q], recv_pair.at[0, q], q, grid),
            remote(code_ref, codes.at[slot], send_pair.at[1, q], recv_pair.at[1, q], q, grid),
        )

    def between_chips(q, from_grid):
        slot = from_grid * owners + q
        return tuple(
            remote(ref.at[slot], ref.at[slot], send_chip.at[i, q], recv_chip.at[i, q], pair, other_chip)
            for i, ref in enumerate((values, codes))
        )

    def between_cores(q, from_grid, turn):
        slot = from_grid * owners + q
        return tuple(
            remote(
                ref.at[slot], ref.at[slot], send_core.at[i, turn, q], recv_core.at[i, turn, q],
                pair, other_core,
            )
            for i, ref in enumerate((values, codes))
        )

    order = [0] + [k for k in range(1, couples) if k != couples // 2] + [couples // 2]
    for k in order:
        zz = lax.rem(z + k, couples)
        start = pl.multiple_of(zz * 2 * width, 2 * width)
        spectra = jnp.dot(
            win[...], table[:, pl.ds(start, 2 * width)], preferred_element_type=jnp.float32
        ).astype(jnp.bfloat16)
        for h in range(2):
            for c in range(comps):
                outbox[2 * zz + h, :, c * width : (c + 1) * width] = spectra[
                    c * rows : (c + 1) * rows, h * width : (h + 1) * width
                ]
        if k == 0:
            own = (
                pltpu.make_async_copy(outbox.at[pair], values.at[mine], own_sems.at[0]),
                pltpu.make_async_copy(code_ref, codes.at[mine], own_sems.at[1]),
            )
            for copy in own:
                copy.start()
            for copy in to_owner(2 * z + 1 - y):
                copy.start()
            for copy in own:
                copy.wait()
            for copy in between_chips(pair, grid) + between_cores(pair, grid, 0):
                copy.start()
        else:
            for h in range(2):
                for copy in to_owner(2 * zz + h):
                    copy.start()

    def pass_on(q):
        for copy in between_chips(q, grid):
            copy.wait_recv()
        for copy in between_cores(q, other_chip, 1):
            copy.start()

    sources = [pair, 2 * z + 1 - y]
    for k in order[1:]:
        back = lax.rem(z + couples - k, couples)
        sources += [2 * back, 2 * back + 1]
    swap = swap_matrix(16)
    clear_gaps(turned, blocks)
    green_steps = [(part, ri) for part in range(freqs // 16) for ri in range(2)]
    for step, q in enumerate(sources):
        turn_green(green_ref, raw, turned, green_sems, swap, *green_steps[step])
        if step > 0:
            for copy in from_source(q):
                copy.wait_recv()
            for copy in between_chips(q, grid) + between_cores(q, grid, 0):
                copy.start()
        if step >= 2:
            pass_on(sources[step - 2])
    for q in sources[len(sources) - 2 :]:
        pass_on(q)
    for q in sources:
        for copy in between_cores(q, grid, 0) + between_cores(q, other_chip, 1):
            copy.wait_recv()

    code_row = jnp.concatenate([codes[i][0:1, 0:rows] for i in range(codes.shape[0])], axis=1)
    couple(code_row, values, blocks, by_lane)
    spread_matrix(by_lane, system)
    parts[pair] = quadratic(system, turned)

    def to_peer(k):
        there = lax.rem(pair + k, owners)
        return remote(parts.at[pair], parts.at[pair], send_part.at[there], recv_part.at[pair], there, grid)

    def from_peer(k):
        there = lax.rem(pair + k, owners)
        return remote(parts.at[there], parts.at[there], send_part.at[there], recv_part.at[there], there, grid)

    for k in range(1, owners):
        to_peer(k).start()
    for k in range(1, owners):
        from_peer(k).wait_recv()
    for band in range(BANDS):
        members = [parts[o] for o in range(owners) if o * freqs // NF == band]
        out_ref[band : band + 1, :] = sum(members[1:], members[0])
    for q in sources:
        for copy in between_chips(q, grid) + between_cores(q, grid, 0) + between_cores(q, other_chip, 1):
            copy.wait_send()
    for q in sources[1:]:
        for copy in to_owner(q):
            copy.wait_send()
    for k in range(1, owners):
        to_peer(k).wait_send()


def fast_body(
    adjoint, first_block, second_station, station_block, lag_lo, lag_hi, pair_count, green_function
):
    rows, comps, lags = adjoint.shape
    blocks, _, _, freqs, points = green_function.shape
    owners, grids = lax.axis_size("pair"), lax.axis_size("grid")
    tables = twiddles(lags, BANDS * NF, NF, owners)
    padded = -(-lags // (8 * STEP)) * (8 * STEP)
    columns = 2 * BANDS * NF
    chunks = owners * grids
    vmem = pl.BlockSpec(memory_space=pltpu.VMEM)
    dma = pltpu.SemaphoreType.DMA
    return pl.pallas_call(
        functools.partial(main_kernel, owners),
        out_shape=jax.ShapeDtypeStruct((BANDS, points), jnp.float32),
        in_specs=[vmem] * 9 + [pl.BlockSpec(memory_space=pl.ANY)],
        out_specs=vmem,
        scratch_shapes=[
            pltpu.VMEM((rows * comps, padded), jnp.bfloat16),
            pltpu.VMEM((padded, columns), jnp.bfloat16),
            pltpu.VMEM((8, 128), jnp.int32),
            pltpu.VMEM((owners, rows, comps * 2 * freqs), jnp.bfloat16),
            pltpu.VMEM((chunks, rows, comps * 2 * freqs), jnp.bfloat16),
            pltpu.VMEM((chunks, 8, 128), jnp.int32),
            pltpu.VMEM((2, blocks, 3, 2, 16, points), jnp.bfloat16),
            pltpu.VMEM((freqs, 256, points), jnp.bfloat16),
            pltpu.VMEM((3 * blocks, 128, 128), jnp.bfloat16),
            pltpu.VMEM((freqs, 6 * blocks, 256), jnp.bfloat16),
            pltpu.VMEM((owners, 1, points), jnp.float32),
            dma((2,)),
            dma((2,)),
            dma((2, owners)),
            dma((2, owners)),
            dma((2, owners)),
            dma((2, owners)),
            dma((2, 2, owners)),
            dma((2, 2, owners)),
            dma((owners,)),
            dma((owners,)),
        ],
        compiler_params=pltpu.CompilerParams(
            collective_id=0, has_side_effects=True, vmem_limit_bytes=60 * 1024 * 1024
        ),
        name="sensitivity",
    )(
        jnp.transpose(adjoint, (1, 0, 2)),
        lag_lo[None, :],
        lag_hi[None, :],
        pair_count[None, :],
        first_block.reshape(1, rows),
        second_station[None, :],
        station_block[None, :],
        *tables,
        green_function,
    )


def solution(mesh):
    placed = (
        P(("pair", "grid"), None, None),
        P(("pair", "grid"), None),
        P(("pair", "grid")),
        P(),
        P(("pair", "grid")),
        P(("pair", "grid")),
        P(("pair", "grid")),
        P(None, None, None, "pair", "grid"),
    )
    local_freqs = BANDS * NF // mesh.shape["pair"]
    return jax.shard_map(
        fast_body if local_freqs == 64 else body, mesh=mesh, in_specs=placed, out_specs=P(None, "grid"), check_vma=False
    )
```
